32 devices in a mesh: half: 2 (over core), cls: 4 (over z), vol: 4 (over y, x).
Axes of the slice: x: 2, y: 2, z: 4, core: 2. Of those that a mesh axis runs over, the one named last changes fastest.
Arguments:
- images: bfloat16 [1024, 16384], P(('half', 'cls'), 'vol')
- groups: int32 [1024, 1], P(('half', 'cls')), may hold values from 0 to 3; in each aligned block of 128 rows (0 to 127, 128 to 255, ...) at most 64 rows name the same one
- references: bfloat16 [128, 16384], P('cls', 'vol'), may hold values from -0.046875 to 0.046875
- interp_index: int32 [128, 16384], P('cls', 'vol'), may hold values from 0 to 2047
- shell_index: int32 [4, 262144], P('vol', ('half', 'cls')), may hold values from 0 to 127
Outputs:
- volume: float32 [4, 262144], P('vol', ('half', 'cls'))
- shell_fsc: float32 [128], replicated
The draws below stay inside these ranges and needn't reach their ends.
Inputs may be any that keep to these rules, and one draw needn't show every extreme that they name: `groups`: within each aligned block of 128 particles no group appears more than 64 times, a bound that some block reaches.
All inputs are finite; a program needn't handle non-finite values.
Results may differ from the reference program's by a relative error of at most 0.00041.
Values may be sent and summed in bfloat16 or wider, within the bound.
A program may use at most 64 MiB of HBM per device.

```python
import math
import jax
import jax.numpy as jnp
import numpy as np
from jax import lax

IMG = 128
SHIFTS = 5
NSHELL = 128
PART_DEV = 128
CLS_DEV = 32
PLANES = 4
VBOX = 256
PIX = 16384
PIXQ = 4096
VOXS = 262144
CAP = 64
CLASSES = 128
PARTICLES = 1024
N_HALF = 2
N_CLS = 4
N_VOL = 4


def draw_images(key, part):
    template_key = jax.random.fold_in(key, 11)
    noise_key = jax.random.fold_in(key, 12)
    columns = jnp.arange(IMG, dtype=jnp.float32)
    amplitude = 1.5 * jnp.exp(-4.0 * columns / IMG)
    template = jax.random.normal(template_key, (IMG, IMG), jnp.float32) * amplitude[None, :]
    noise = jax.random.normal(noise_key, (PARTICLES, IMG, IMG), jnp.float32)
    values = template[None, :, :] + noise
    values = jnp.clip(values, -8.0, 8.0)
    return values.reshape(PARTICLES, IMG * IMG).astype(jnp.bfloat16)


def draw_interp_index(key, part):
    band_key = jax.random.fold_in(key, 21)
    depth_key = jax.random.fold_in(key, 22)
    depth = VBOX * PLANES
    band = jax.random.randint(band_key, (CLASSES, IMG * IMG), 0, 2, jnp.int32)
    offset = jax.random.randint(depth_key, (CLASSES, IMG * IMG), 0, depth, jnp.int32)
    return (band * depth + offset).astype(jnp.int32)


def draw_shell_index(key, part):
    jitter_key = jax.random.fold_in(key, 31)
    depth = VBOX * PLANES
    radius = jnp.arange(VOXS, dtype=jnp.int32) // depth
    base = radius * NSHELL // VBOX
    jitter = jax.random.randint(jitter_key, (N_VOL, VOXS), 0, max(NSHELL // 16, 2), jnp.int32)
    return jnp.minimum(base[None, :] + jitter, NSHELL - 1).astype(jnp.int32)


def levels(stream_key, dims, cuts, smallest, high):
    gain, own = 1.0, jax.random.fold_in(stream_key, 6)
    for position, blocks in cuts:
        heights = jnp.exp(jax.random.uniform(jax.random.fold_in(own, position), (blocks,), jnp.float32, smallest / len(cuts), high / len(cuts)))
        gain = gain * jnp.repeat(heights, dims[position] // blocks).reshape([-1 if axis == position else 1 for axis in range(len(dims))])
    return gain


def shared_out(rng, own, number, rows, amount, top, limit, lean):
    sequence = jax.random.permutation(rng, amount)
    heavy_load, ordinary = shares(amount, rows * top, limit, lean, True), shares(amount, rows * top, limit, lean, False)
    places = jnp.arange(amount)

    def named(sizes, offset_by):
        used = int((sizes > 0).sum())
        fixed = max(1, used // 4)
        moved = fixed + (places - fixed + offset_by * (used - fixed)) % max(1, amount - fixed)
        return jnp.zeros((amount,), jnp.int32).at[sequence[jnp.where(places < fixed, places, moved)]].set(jnp.asarray(sizes, jnp.int32))

    sizes = jnp.where(number % 4 == 0, named(heavy_load, number // 4), named(ordinary, number - number // 4 - 1))
    mixed = jax.random.permutation(jax.random.fold_in(own, 3), amount)
    donor, taker = mixed[0:amount // 2 * 2:2], mixed[1:amount // 2 * 2:2]
    room = jnp.minimum(sizes[donor] - 1, limit - sizes[taker]) // 2
    room = jnp.where((donor == sequence[0]) | (taker == sequence[0]) | (sizes[taker] == 0), 0, jnp.maximum(room, 0))
    moved = jax.random.randint(jax.random.fold_in(own, 4), (amount // 2,), 0, 1 << 20) % (room + 1)
    sizes = sizes.at[donor].add(-moved).at[taker].add(moved)
    labels = jnp.searchsorted(jnp.cumsum(sizes), jnp.arange(rows * top), side="right").astype(jnp.int32)
    grid = labels.reshape(top, rows).T
    grid = grid[jax.random.permutation(jax.random.fold_in(own, 1), rows)]
    offset_by = jax.random.randint(jax.random.fold_in(own, 2), (rows, 1), 0, top)
    return jnp.take_along_axis(grid, (jnp.arange(top)[None, :] + offset_by) % top, axis=1)


def shares(count, total, bound, lean, full):
    weights = [(1 << 20) // math.isqrt(standing ** lean) + 1 for standing in range(1, count + 1)]
    largest = bound if full else min(bound, max(-(-total // count), total * weights[0] // sum(weights)))
    least = 1 if total - largest >= count - 1 else 0
    given, rest = [largest] + [least] * (count - 1), total - largest - least * (count - 1)
    while rest > 0:
        free = [i for i in range(1, count) if given[i] < largest] or [i for i in range(1, count) if given[i] < bound]
        pool, budget = sum([weights[i] for i in free]), rest
        for i in free:
            more = min(bound - given[i], max(1, budget * weights[i] // pool), rest)
            given[i] = given[i] + more
            rest = rest - more
    return np.array(given)


def gaussian(rng, dims, spread, bound, split=(), kind=jnp.bfloat16):
    array = jax.random.normal(rng, dims, jnp.float32) * spread
    if len(split) > 0:
        array = levels(rng, dims, split, -0.22, 0.18) * array
    return jnp.clip(array, min=-bound, max=bound).astype(kind)


def setup_inputs(seed: int = 0) -> dict:
    keys = jax.random.split(jax.random.key(seed), 6)
    images = draw_images(jax.random.fold_in(keys[5], 71), 0)
    groups_keys = jax.random.split(jax.random.fold_in(keys[1], 1), PARTICLES // PART_DEV)
    groups_turns = jax.random.permutation(jax.random.fold_in(keys[1], 3), PARTICLES // PART_DEV)
    groups = jax.vmap(lambda own, number: shared_out(jax.random.fold_in(keys[1], 2), own, number, PART_DEV, N_CLS, 1, CAP, 2))(groups_keys, groups_turns).reshape((PARTICLES, 1))
    references = gaussian(keys[2], (CLASSES, PIX), PIX ** -0.5, 0.046875, ((0, 4), (1, 4)))
    interp_index = draw_interp_index(jax.random.fold_in(keys[5], 71), 0)
    shell_index = draw_shell_index(jax.random.fold_in(keys[5], 71), 0)
    return {"images": images, "groups": groups, "references": references, "interp_index": interp_index, "shell_index": shell_index}


EPS_W = 1e-05
EPS_F = 1e-06

def slab_sum(values, targets):
    column_ids = jnp.arange(PIXQ, dtype=jnp.int32) % IMG
    placed = targets + 2 * VBOX * PLANES * column_ids[None, :]
    return jax.ops.segment_sum(values.reshape(-1), placed.reshape(-1), num_segments=VOXS)

def owner_step(carry, inputs, images):
    slot_rows, owner_refs, owner_interp = inputs
    filled = slot_rows >= 0
    picked = jnp.take(images, jnp.maximum(slot_rows, 0), axis=0)
    picked = jnp.where(filled[:, None], picked, jnp.zeros((), images.dtype))
    rolled = jnp.concatenate([jnp.roll(owner_refs, -(shift_id - SHIFTS // 2), axis=2).reshape(CLS_DEV, PIX) for shift_id in range(SHIFTS)], axis=0)
    scores = jnp.dot(picked, rolled.T, preferred_element_type=jnp.float32)
    mean_square = lax.optimization_barrier(jnp.mean(scores * scores, axis=1, keepdims=True))
    weights = (scores * scores / (mean_square + EPS_W)).astype(jnp.bfloat16)
    summed = jnp.dot(weights.T, picked, preferred_element_type=jnp.float32).reshape(SHIFTS, CLS_DEV, IMG, IMG)
    aligned = jnp.roll(summed[0], -(SHIFTS // 2), axis=2)
    for shift_id in range(1, SHIFTS):
        aligned = aligned + jnp.roll(summed[shift_id], shift_id - SHIFTS // 2, axis=2)
    aligned = aligned.reshape(CLS_DEV, N_VOL, PIXQ)
    added = jax.vmap(slab_sum, in_axes=(1, 1))(aligned, owner_interp)
    return (carry + added, None)

def reference(images, groups, references, interp_index, shell_index):
    slot_total = N_CLS * CAP
    blocks = groups[:, 0].reshape(N_HALF * N_CLS, PART_DEV)
    matches = (blocks[:, :, None] == jnp.arange(N_CLS, dtype=jnp.int32)[None, None, :]).astype(jnp.int32)
    order_in = lax.optimization_barrier(jnp.sum(jnp.cumsum(matches, axis=1) * matches, axis=2)) - 1
    block_ids = jnp.arange(N_HALF * N_CLS, dtype=jnp.int32)
    halves = block_ids // N_CLS
    sources = block_ids % N_CLS
    target = (halves[:, None] * N_CLS + blocks) * slot_total + sources[:, None] * CAP + order_in
    table = jnp.full((N_HALF * N_CLS * slot_total,), -1, jnp.int32)
    table = table.at[target.reshape(-1).astype(jnp.int32)].set(jnp.arange(PARTICLES, dtype=jnp.int32))
    table = table.reshape(N_HALF, N_CLS, slot_total)
    grouped_refs = references.reshape(N_CLS, CLS_DEV, IMG, IMG)
    grouped_interp = interp_index.reshape(N_CLS, CLS_DEV, N_VOL, PIXQ)
    maps = []
    for half_id in range(N_HALF):
        start = jnp.zeros((N_VOL, VOXS), jnp.float32)
        half_map, _ = lax.scan(lambda carry, inputs: owner_step(carry, inputs, images), start, (table[half_id], grouped_refs, grouped_interp))
        maps.append(half_map)
    first, second = (maps[0], maps[1])
    flat_shells = shell_index.reshape(-1)
    sq_first = jax.ops.segment_sum((first * first).reshape(-1), flat_shells, num_segments=NSHELL)
    sq_second = jax.ops.segment_sum((second * second).reshape(-1), flat_shells, num_segments=NSHELL)
    cross = jax.ops.segment_sum((first * second).reshape(-1), flat_shells, num_segments=NSHELL)
    shell_fsc = cross / (jnp.sqrt(sq_first) * jnp.sqrt(sq_second) + EPS_F)
    mean_sq = (jnp.sum(sq_first) + jnp.sum(sq_second) + 2.0 * jnp.sum(cross)) / (4.0 * N_VOL * VOXS)
    volume = jnp.take(shell_fsc, shell_index) * (0.5 * (first + second)) / jnp.sqrt(mean_sq + EPS_F)
    return (volume, shell_fsc)
```

```python
import functools

import jax
import jax.numpy as jnp
from jax import lax
from jax.experimental import pallas as pl
from jax.experimental.pallas import tpu as pltpu
from jax.sharding import PartitionSpec as P

IMG = 128
SHIFTS = 5
NSHELL = 128
PLANES = 4
VBOX = 256
VOXS = 262144


EPS_W = 1e-05
EPS_F = 1e-06


def partner(shard, axis, apart):
    return lax.ppermute(shard, axis, [(i, i ^ 1 << apart) for i in range(lax.axis_size(axis))])


def insert_body(place_ref, value_ref, out_ref):
    cols, count = place_ref.shape
    chunk = min(count, 1024)
    low_ids = lax.broadcasted_iota(jnp.int32, (128, chunk), 0)
    high_ids = lax.broadcasted_iota(jnp.int32, (16, chunk), 0)
    for col in range(cols):
        total = jnp.zeros((32, 128), jnp.float32)
        for start in range(0, count, chunk):
            place = place_ref[col : col + 1, start : start + chunk]
            value = value_ref[col : col + 1, start : start + chunk]
            coarse = value.astype(jnp.bfloat16).astype(jnp.float32)
            fine = value - coarse
            hit = high_ids == (place >> 7)
            left = jnp.concatenate(
                [jnp.where(hit, coarse, 0.0), jnp.where(hit, fine, 0.0)], axis=0
            ).astype(jnp.bfloat16)
            right = jnp.where(low_ids == (place & 127), 1.0, 0.0).astype(jnp.bfloat16)
            total += lax.dot_general(
                left, right, (((1,), (1,)), ((), ())), preferred_element_type=jnp.float32
            )
        out_ref[col] = total[:16] + total[16:]


def insert(place, value):
    cols, count = place.shape
    step = 8
    return pl.pallas_call(
        insert_body,
        grid=(cols // step,),
        in_specs=[pl.BlockSpec((step, count), lambda i: (i, 0))] * 2,
        out_specs=pl.BlockSpec((step, 16, 128), lambda i: (i, 0, 0)),
        out_shape=jax.ShapeDtypeStruct((cols, 16, 128), jnp.float32),
        compiler_params=pltpu.CompilerParams(vmem_limit_bytes=32 << 20),
    )(place, value)


def fused_body(
    n_cls, n_vol, images, refs, places, groups, shells, volume, fsc_out,
    rolled, refs_all, places_all, places32, scores, score_box, flipped, by_col, by_col_in,
    slab, slab_in, hot, stat_half, stat_cls, stat_vol,
    ref_send, ref_recv, fwd_send, fwd_recv, place_send, place_recv, score_send, score_recv,
    half_send, half_recv, slab_send, slab_recv, stat_send, stat_recv,
):
    half, cls, vol = lax.axis_index("half"), lax.axis_index("cls"), lax.axis_index("vol")
    other = 1 - half
    part_count, pix = images.shape
    class_count = refs.shape[0]
    split = class_count // 2
    cols = IMG // 2
    own_cols = cols // n_cls
    mine = (half, cls, vol)

    def along(axis, step):
        at = list(mine)
        at[axis] = lax.rem(mine[axis] + step, (2, n_cls, n_vol)[axis])
        return tuple(at)

    def push(src, dst, send, recv, target):
        return pltpu.make_async_remote_copy(
            src_ref=src, dst_ref=dst, send_sem=send, recv_sem=recv,
            device_id=target, device_id_type=pl.DeviceIdType.MESH,
        )

    peers = [along(0, 1)]
    peers += [along(1, t) for t in range(1, n_cls)] + [along(2, t) for t in range(1, n_vol)]
    barrier = pltpu.get_barrier_semaphore()
    for peer in peers:
        pl.semaphore_signal(barrier, inc=1, device_id=peer, device_id_type=pl.DeviceIdType.MESH)
    pl.semaphore_wait(barrier, len(peers))

    ref_copies, place_copies, fwd_copies = [], [], []
    for t in range(1, n_cls):
        ref_copies.append(push(
            refs.at[pl.ds(half * split, split)],
            refs_all.at[pl.ds(cls * class_count + half * split, split)],
            ref_send.at[t - 1], ref_recv.at[t - 1], along(1, t),
        ))
        ref_copies[-1].start()
    for t in range(1, n_cls):
        place_copies.append(push(
            places.at[pl.ds(half * cols, cols)], places_all.at[cls],
            place_send.at[t - 1], place_recv.at[t - 1], along(1, t),
        ))
        place_copies[-1].start()
    refs_all[pl.ds(cls * class_count, class_count), :] = refs[...]

    def roll_rows(r, carry):
        at = pl.ds(pl.multiple_of(r * IMG, IMG), IMG)
        band = images[:, at].astype(jnp.float32)
        for i in range(SHIFTS):
            turned = pltpu.roll(band, (i - SHIFTS // 2) % IMG, 1)
            rolled[i * part_count : (i + 1) * part_count, at] = turned.astype(jnp.bfloat16)
        return carry

    lax.fori_loop(0, pix // IMG, roll_rows, 0)

    for t in range(1, n_cls):
        ref_copies[t - 1].wait_recv()
        source = lax.rem(cls - t + n_cls, n_cls)
        rows = pl.ds(source * class_count + half * split, split)
        fwd_copies.append(push(
            refs_all.at[rows], refs_all.at[rows], fwd_send.at[t - 1], fwd_recv.at[t - 1], along(0, 1)
        ))
        fwd_copies[-1].start()
    for copy in fwd_copies:
        copy.wait_recv()

    scores[...] = jnp.zeros_like(scores)

    def score_step(m, carry):
        at = pl.ds(pl.multiple_of(m * 512, 512), 512)
        scores[...] += lax.dot_general(
            rolled[:, at], refs_all[:, at], (((1,), (1,)), ((), ())),
            preferred_element_type=jnp.float32,
        )
        return carry

    lax.fori_loop(0, pix // 512, score_step, 0)

    lanes = 4 * class_count
    lane_block = lax.broadcasted_iota(jnp.int32, (part_count, lanes), 1) // class_count
    own_group = groups[...] == lane_block

    def spread(x):
        x = x + pltpu.roll(x, lanes // 2, 1)
        return x + pltpu.roll(x, lanes // 4, 1)

    packed = jnp.zeros((part_count, lanes), jnp.float32)
    for i in range(4):
        part = jnp.where(own_group, scores[i * part_count : (i + 1) * part_count, :], 0.0)
        packed = jnp.where(lane_block == i, spread(part), packed)
    last = spread(jnp.where(own_group, scores[4 * part_count :, :], 0.0))
    quarter = part_count // 4
    tail = jnp.zeros((quarter, lanes), jnp.float32)
    for b in range(4):
        tail = jnp.where(lane_block[:quarter] == b, last[b * quarter : (b + 1) * quarter], tail)
    score_box[vol, 0:part_count, :] = packed
    score_box[vol, part_count : part_count + quarter, :] = tail
    score_copies = []
    for t in range(1, n_vol):
        score_copies.append(push(
            score_box.at[vol], score_box.at[vol], score_send.at[t - 1], score_recv.at[t - 1], along(2, t)
        ))
        score_copies[-1].start()
    for copy in score_copies:
        copy.wait()
    summed = score_box[0]
    for v in range(1, n_vol):
        summed = summed + score_box[v]
    packed, tail = summed[:part_count], summed[part_count:]
    squares = []
    for i in range(4):
        part = spread(jnp.where(lane_block == i, packed, 0.0))
        squares.append(part * part)
    last = jnp.concatenate(
        [spread(jnp.where(lane_block[:quarter] == b, tail, 0.0)) for b in range(4)], axis=0
    )
    squares.append(last * last)
    total = squares[0]
    for i in range(1, SHIFTS):
        total = total + squares[i]
    mean_square = jnp.sum(total, axis=1, keepdims=True) * (1.0 / (4 * SHIFTS * class_count))
    for i in range(SHIFTS):
        weight = jnp.where(own_group, squares[i] / (mean_square + EPS_W), 0.0)
        flipped[:, i * part_count : (i + 1) * part_count] = weight.T.astype(jnp.bfloat16)

    tiles = pix // IMG // 4

    def sum_step(m, carry):
        block = lax.dot_general(
            flipped[...], rolled[:, pl.ds(pl.multiple_of(m * 4 * IMG, 4 * IMG), 4 * IMG)],
            (((1,), (0,)), ((), ())), preferred_element_type=jnp.float32,
        )
        for g in range(n_cls):
            tile = jnp.concatenate(
                [
                    block[g * class_count : (g + 1) * class_count, r * IMG : (r + 1) * IMG]
                    for r in range(4)
                ],
                axis=0,
            )
            at = pl.ds(pl.multiple_of((g * tiles + m) * IMG, IMG), IMG)
            by_col[:, at] = tile.T
        return carry

    lax.fori_loop(0, tiles, sum_step, 0)
    half_copy = push(
        by_col.at[pl.ds(other * cols, cols)], by_col_in, half_send.at[0], half_recv.at[0], along(0, 1)
    )
    half_copy.start()
    for copy in place_copies:
        copy.wait_recv()
    places32[cls] = places[pl.ds(pl.multiple_of(half * cols, cols), cols), :].astype(jnp.int32)
    for t in range(1, n_cls):
        source = lax.rem(cls - t + n_cls, n_cls)
        places32[source] = places_all[source].astype(jnp.int32)
    half_copy.wait()

    chunk = places.shape[1]
    low_ids = lax.broadcasted_iota(jnp.int32, (128, chunk), 0)
    high_ids = lax.broadcasted_iota(jnp.int32, (16, chunk), 0)

    def insert_eight(target, eight):
        base = pl.multiple_of(target * own_cols + eight * 8, 8)
        for j in range(8):
            total = jnp.zeros((64, 128), jnp.float32)
            for g in range(n_cls):
                span = slice(g * chunk, (g + 1) * chunk)
                place = places32[g, pl.ds(base, 8), :][j : j + 1]
                own = by_col[pl.ds(pl.multiple_of(half * cols + base, 8), 8), span][j : j + 1]
                got = by_col_in[pl.ds(base, 8), span][j : j + 1]
                hit = high_ids == (place >> 7)
                parts = []
                for value in (own, got):
                    coarse = value.astype(jnp.bfloat16).astype(jnp.float32)
                    fine = value - coarse
                    parts += [jnp.where(hit, coarse, 0.0), jnp.where(hit, fine, 0.0)]
                left = jnp.concatenate(parts, axis=0).astype(jnp.bfloat16)
                right = jnp.where(low_ids == (place & 127), 1.0, 0.0).astype(jnp.bfloat16)
                total += lax.dot_general(
                    left, right, (((1,), (1,)), ((), ())), preferred_element_type=jnp.float32
                )
            rows = pl.ds(pl.multiple_of(eight * 128 + j * 16, 16), 16)
            slab[target, 0, rows, :] = total[0:16] + total[16:32]
            slab[target, 1, rows, :] = total[32:48] + total[48:64]

    slab_copies = []
    for t in range(1, n_cls + 1):
        target = lax.rem(cls + t, n_cls)

        def eight_step(e, carry, target=target):
            insert_eight(target, e)
            return carry

        lax.fori_loop(0, own_cols // 8, eight_step, 0)
        if t < n_cls:
            slab_copies.append(push(
                slab.at[target], slab_in.at[t - 1], slab_send.at[t - 1], slab_recv.at[t - 1], along(1, t)
            ))
            slab_copies[-1].start()
    for copy in slab_copies:
        copy.wait()

    shell_ids = lax.broadcasted_iota(jnp.int32, (NSHELL, 128), 0)
    blank = jnp.zeros((1, 128), jnp.float32)

    def stat_step(m, carry):
        rows = pl.ds(pl.multiple_of(m * 8, 8), 8)
        maps = []
        for k in range(2):
            x = slab[cls, k, rows, :]
            for t in range(1, n_cls):
                x = x + slab_in[t - 1, k, rows, :]
            maps.append(x)
            slab[cls, k, rows, :] = x
        terms = []
        for x in (maps[0] * maps[0], maps[1] * maps[1], maps[0] * maps[1]):
            coarse = x.astype(jnp.bfloat16).astype(jnp.float32)
            terms += [coarse, x - coarse]
        shell = shells[rows, :]
        left = jnp.concatenate(
            [
                jnp.concatenate([x[j : j + 1] for x in terms] + [blank, blank], axis=0)
                for j in range(8)
            ],
            axis=1,
        ).astype(jnp.bfloat16)
        right = jnp.concatenate(
            [
                jnp.where(shell_ids == shell[j : j + 1], 1.0, 0.0).astype(jnp.bfloat16)
                for j in range(8)
            ],
            axis=1,
        )
        hot[m] = right
        return carry + lax.dot_general(
            left, right, (((1,), (1,)), ((), ())), preferred_element_type=jnp.float32
        )

    blocks = shells.shape[0] // 8
    sums = lax.fori_loop(0, blocks, stat_step, jnp.zeros((8, NSHELL), jnp.float32))
    mine_sq, other_sq, cross = sums[0:1] + sums[1:2], sums[2:3] + sums[3:4], sums[4:5] + sums[5:6]
    row_ids = lax.broadcasted_iota(jnp.int32, (8, NSHELL), 0)
    swap = jnp.full((1, NSHELL), half, jnp.int32) == 1
    first_sq = jnp.where(swap, other_sq, mine_sq)
    second_sq = jnp.where(swap, mine_sq, other_sq)
    stat = jnp.where(row_ids == 0, first_sq, jnp.where(row_ids == 1, second_sq, cross))
    at = 0
    for axis, box in enumerate((stat_half, stat_cls, stat_vol)):
        size = box.shape[0]
        box[mine[axis]] = stat
        copies = []
        for t in range(1, size):
            copies.append(push(
                box.at[mine[axis]], box.at[mine[axis]], stat_send.at[at], stat_recv.at[at], along(axis, t)
            ))
            copies[-1].start()
            at += 1
        for copy in copies:
            copy.wait()
        stat = box[0]
        for k in range(1, size):
            stat = stat + box[k]
    first_sq, second_sq, cross = stat[0:1], stat[1:2], stat[2:3]
    fsc = cross / (jnp.sqrt(first_sq) * jnp.sqrt(second_sq) + EPS_F)
    fsc_out[...] = fsc
    mean_sq = jnp.sum(first_sq + second_sq + 2.0 * cross, axis=1, keepdims=True) * (
        1.0 / (4.0 * n_vol * VOXS)
    )
    scale = 0.5 / jnp.sqrt(mean_sq + EPS_F)
    coarse = fsc.astype(jnp.bfloat16).astype(jnp.float32)
    pair = jnp.where(row_ids == 0, coarse, jnp.where(row_ids == 1, fsc - coarse, 0.0)).astype(jnp.bfloat16)

    def volume_step(m, carry):
        rows = pl.ds(pl.multiple_of(m * 8, 8), 8)
        picked = jnp.dot(pair, hot[m], preferred_element_type=jnp.float32)
        picked = picked[0:1] + picked[1:2]
        weight = jnp.concatenate([picked[:, j * 128 : (j + 1) * 128] for j in range(8)], axis=0)
        volume[rows, :] = weight * (slab[cls, 0, rows, :] + slab[cls, 1, rows, :]) * scale
        return carry

    lax.fori_loop(0, blocks, volume_step, 0)
    for copy in ref_copies + place_copies + fwd_copies:
        copy.wait_send()


def fused(images, groups, references, interp_index, shell_index):
    n_cls, n_vol = lax.axis_size("cls"), lax.axis_size("vol")
    part_count, pix = images.shape
    class_count = references.shape[0]
    rows = pix // IMG
    piece = shell_index.shape[1] // 128
    places = jnp.transpose(interp_index.astype(jnp.int16).reshape(class_count, rows, IMG), (2, 1, 0))
    places = places.reshape(IMG, rows * class_count)
    lanes = n_cls * class_count
    count = rows * class_count
    half_cols = IMG // 2
    dma = pltpu.SemaphoreType.DMA
    bf16, f32 = jnp.bfloat16, jnp.float32
    volume, fsc = pl.pallas_call(
        functools.partial(fused_body, n_cls, n_vol),
        out_shape=(
            jax.ShapeDtypeStruct((piece, 128), f32),
            jax.ShapeDtypeStruct((1, NSHELL), f32),
        ),
        in_specs=[pl.BlockSpec(memory_space=pltpu.VMEM)] * 5,
        out_specs=(pl.BlockSpec(memory_space=pltpu.VMEM),) * 2,
        scratch_shapes=[
            pltpu.VMEM((SHIFTS * part_count, pix), bf16),
            pltpu.VMEM((lanes, pix), bf16),
            pltpu.VMEM((n_cls, half_cols, count), jnp.int16),
            pltpu.VMEM((n_cls, half_cols, count), jnp.int32),
            pltpu.VMEM((SHIFTS * part_count, lanes), f32),
            pltpu.VMEM((n_vol, part_count + part_count // 4, lanes), f32),
            pltpu.VMEM((lanes, SHIFTS * part_count), bf16),
            pltpu.VMEM((IMG, n_cls * count), f32),
            pltpu.VMEM((half_cols, n_cls * count), f32),
            pltpu.VMEM((n_cls, 2, piece, 128), f32),
            pltpu.VMEM((n_cls - 1, 2, piece, 128), f32),
            pltpu.VMEM((piece // 8, NSHELL, 1024), bf16),
            pltpu.VMEM((2, 8, NSHELL), f32),
            pltpu.VMEM((n_cls, 8, NSHELL), f32),
            pltpu.VMEM((n_vol, 8, NSHELL), f32),
        ]
        + [dma((n_cls - 1,))] * 6
        + [dma((n_vol - 1,))] * 2
        + [dma((1,))] * 2
        + [dma((n_cls - 1,))] * 2
        + [dma((n_cls + n_vol - 1,))] * 2,
        compiler_params=pltpu.CompilerParams(
            collective_id=0, has_side_effects=True, vmem_limit_bytes=56 << 20
        ),
    )(images, references, places, groups, shell_index.reshape(piece, 128))
    return (volume.reshape(1, -1), fsc[0])


def shards(images, groups, references, interp_index, shell_index):
    n_cls = lax.axis_size("cls")
    n_vol = lax.axis_size("vol")
    n_half = lax.axis_size("half")
    part_count, pix_quarter = images.shape
    class_count = references.shape[0]
    if n_half == 2 and n_cls == 4 and class_count == 32:
        return fused(images, groups, references, interp_index, shell_index)
    capacity = max(2 * part_count // n_cls, 4)
    slot_count = n_cls * capacity
    owner_ids = groups[:, 0]
    same = owner_ids[:, None] == owner_ids[None, :]
    earlier = jnp.arange(part_count)[None, :] < jnp.arange(part_count)[:, None]
    order_in = jnp.sum((same & earlier).astype(jnp.int32), axis=1)
    slot_ids = owner_ids * capacity + order_in
    slot_hits = slot_ids[None, :] == jnp.arange(slot_count, dtype=jnp.int32)[:, None]
    source_ids = jnp.sum(
        jnp.where(slot_hits, jnp.arange(part_count, dtype=jnp.int32)[None, :], 0), axis=1
    )
    filled = jnp.any(slot_hits, axis=1)
    outgoing = jnp.where(
        filled[:, None], jnp.take(images, source_ids, axis=0), jnp.zeros((), jnp.bfloat16)
    )
    arrived = lax.all_to_all(
        outgoing.reshape(n_cls, capacity, pix_quarter),
        "cls",
        split_axis=0,
        concat_axis=0,
        tiled=True,
    )
    arrived = arrived.reshape(slot_count, pix_quarter)
    quarter_rows = pix_quarter // IMG
    shaped_refs = references.reshape(class_count, quarter_rows, IMG)
    rolled_refs = jnp.concatenate(
        [
            jnp.roll(shaped_refs, -(shift_id - SHIFTS // 2), axis=2).reshape(
                class_count, pix_quarter
            )
            for shift_id in range(SHIFTS)
        ],
        axis=0,
    )
    partial_scores = lax.dot_general(
        arrived, rolled_refs, (((1,), (1,)), ((), ())), preferred_element_type=jnp.float32
    )
    partial_scores = partial_scores.reshape(slot_count, SHIFTS, class_count)
    scores = lax.psum(partial_scores, "vol")
    squares = scores * scores
    mean_square = jnp.mean(squares, axis=(1, 2), keepdims=True)
    weights = (squares / (mean_square + EPS_W)).astype(jnp.bfloat16)
    weighted = lax.dot_general(
        weights.reshape(slot_count, SHIFTS * class_count),
        arrived,
        (((0,), (0,)), ((), ())),
        preferred_element_type=jnp.float32,
    )
    weighted = weighted.reshape(SHIFTS, class_count, quarter_rows, IMG)
    aligned = jnp.roll(weighted[0], -(SHIFTS // 2), axis=2)
    for shift_id in range(1, SHIFTS):
        aligned = aligned + jnp.roll(weighted[shift_id], shift_id - SHIFTS // 2, axis=2)
    by_column = jnp.transpose(interp_index.reshape(-1, IMG))
    slab_part = insert(by_column, jnp.transpose(aligned.reshape(-1, IMG)))
    piece_len = VOXS // (n_half * n_cls)
    slab_part = jnp.transpose(slab_part.reshape(n_half, n_cls, piece_len), (1, 0, 2)).reshape(-1)
    block_len = VOXS // n_cls
    slab_full = lax.psum(slab_part, "cls")
    own_block = lax.dynamic_slice_in_dim(slab_full, lax.axis_index("cls") * block_len, block_len)
    half_id = lax.axis_index("half")
    own_piece = lax.dynamic_slice_in_dim(own_block, half_id * piece_len, piece_len)
    other_piece = lax.dynamic_slice_in_dim(own_block, (1 - half_id) * piece_len, piece_len)
    mirror_piece = partner(other_piece, "half", 0)
    first = jnp.where(half_id == 0, own_piece, mirror_piece)
    second = jnp.where(half_id == 0, mirror_piece, own_piece)
    shell_hot = (shell_index[0][:, None] == jnp.arange(NSHELL, dtype=jnp.int32)[None, :]).astype(
        jnp.float32
    )
    stats = jnp.stack([first * first, second * second, first * second])
    shell_terms = jnp.dot(stats, shell_hot, precision=lax.Precision.HIGHEST)
    shell_sums = lax.psum(shell_terms, ("half", "cls", "vol"))
    shell_fsc = shell_sums[2] / (jnp.sqrt(shell_sums[0]) * jnp.sqrt(shell_sums[1]) + EPS_F)
    mean_sq = (jnp.sum(shell_sums[0]) + jnp.sum(shell_sums[1]) + 2.0 * jnp.sum(shell_sums[2])) / (
        4.0 * n_vol * VOXS
    )
    filter_vox = jnp.dot(shell_hot, shell_fsc, precision=lax.Precision.HIGHEST)
    volume = filter_vox * (0.5 * (first + second)) / jnp.sqrt(mean_sq + EPS_F)
    return (volume[None, :], shell_fsc)


def solution(mesh):
    placed = (
        P(("half", "cls"), "vol"),
        P(("half", "cls"), None),
        P("cls", "vol"),
        P("cls", "vol"),
        P("vol", ("half", "cls")),
    )
    return jax.shard_map(
        shards,
        mesh=mesh,
        in_specs=placed,
        out_specs=(P("vol", ("half", "cls")), P()),
        check_vma=False,
    )
```

```python
import functools

import jax
import jax.numpy as jnp
from jax import lax
from jax.experimental import pallas as pl
from jax.experimental.pallas import tpu as pltpu
from jax.sharding import PartitionSpec as P

IMG = 128
SHIFTS = 5
NSHELL = 128
PLANES = 4
VBOX = 256
VOXS = 262144


EPS_W = 1e-05
EPS_F = 1e-06


def partner(shard, axis, apart):
    return lax.ppermute(shard, axis, [(i, i ^ 1 << apart) for i in range(lax.axis_size(axis))])


def insert_body(place_ref, value_ref, out_ref):
    cols, count = place_ref.shape
    chunk = min(count, 1024)
    low_ids = lax.broadcasted_iota(jnp.int32, (128, chunk), 0)
    high_ids = lax.broadcasted_iota(jnp.int32, (16, chunk), 0)
    for col in range(cols):
        total = jnp.zeros((32, 128), jnp.float32)
        for start in range(0, count, chunk):
            place = place_ref[col : col + 1, start : start + chunk]
            value = value_ref[col : col + 1, start : start + chunk]
            coarse = value.astype(jnp.bfloat16).astype(jnp.float32)
            fine = value - coarse
            hit = high_ids == (place >> 7)
            left = jnp.concatenate(
                [jnp.where(hit, coarse, 0.0), jnp.where(hit, fine, 0.0)], axis=0
            ).astype(jnp.bfloat16)
            right = jnp.where(low_ids == (place & 127), 1.0, 0.0).astype(jnp.bfloat16)
            total += lax.dot_general(
                left, right, (((1,), (1,)), ((), ())), preferred_element_type=jnp.float32
            )
        out_ref[col] = total[:16] + total[16:]


def insert(place, value):
    cols, count = place.shape
    step = 8
    return pl.pallas_call(
        insert_body,
        grid=(cols // step,),
        in_specs=[pl.BlockSpec((step, count), lambda i: (i, 0))] * 2,
        out_specs=pl.BlockSpec((step, 16, 128), lambda i: (i, 0, 0)),
        out_shape=jax.ShapeDtypeStruct((cols, 16, 128), jnp.float32),
        compiler_params=pltpu.CompilerParams(vmem_limit_bytes=32 << 20),
    )(place, value)


def fused_body(
    n_cls, n_vol, images, refs, places, groups, shells, volume, fsc_out,
    rolled, refs_all, places_all, places32, scores, score_box, flipped, by_col, by_col_in,
    slab, slab_in, hot, stat_half, stat_cls, stat_vol,
    ref_send, ref_recv, fwd_send, fwd_recv, place_send, place_recv, score_send, score_recv,
    half_send, half_recv, slab_send, slab_recv, stat_send, stat_recv,
):
    half, cls, vol = lax.axis_index("half"), lax.axis_index("cls"), lax.axis_index("vol")
    other = 1 - half
    part_count, pix = images.shape
    class_count = refs.shape[0]
    split = class_count // 2
    cols = IMG // 2
    own_cols = cols // n_cls
    mine = (half, cls, vol)

    def along(axis, step):
        at = list(mine)
        at[axis] = lax.rem(mine[axis] + step, (2, n_cls, n_vol)[axis])
        return tuple(at)

    def push(src, dst, send, recv, target):
        return pltpu.make_async_remote_copy(
            src_ref=src, dst_ref=dst, send_sem=send, recv_sem=recv,
            device_id=target, device_id_type=pl.DeviceIdType.MESH,
        )

    peers = [along(0, 1)]
    peers += [along(1, t) for t in range(1, n_cls)] + [along(2, t) for t in range(1, n_vol)]
    barrier = pltpu.get_barrier_semaphore()
    for peer in peers:
        pl.semaphore_signal(barrier, inc=1, device_id=peer, device_id_type=pl.DeviceIdType.MESH)
    pl.semaphore_wait(barrier, len(peers))

    ref_copies, place_copies, fwd_copies = [], [], []
    for t in range(1, n_cls):
        ref_copies.append(push(
            refs.at[pl.ds(half * split, split)],
            refs_all.at[pl.ds(cls * class_count + half * split, split)],
            ref_send.at[t - 1], ref_recv.at[t - 1], along(1, t),
        ))
        ref_copies[-1].start()
    refs_all[pl.ds(cls * class_count, class_count), :] = refs[...]

    def roll_rows(r, carry):
        at = pl.ds(pl.multiple_of(r * IMG, IMG), IMG)
        band = images[:, at].astype(jnp.float32)
        for i in range(SHIFTS):
            turned = pltpu.roll(band, (i - SHIFTS // 2) % IMG, 1)
            rolled[i * part_count : (i + 1) * part_count, at] = turned.astype(jnp.bfloat16)
        return carry

    lax.fori_loop(0, pix // IMG, roll_rows, 0)

    for t in range(1, n_cls):
        ref_copies[t - 1].wait_recv()
        source = lax.rem(cls - t + n_cls, n_cls)
        rows = pl.ds(source * class_count + half * split, split)
        fwd_copies.append(push(
            refs_all.at[rows], refs_all.at[rows], fwd_send.at[t - 1], fwd_recv.at[t - 1], along(0, 1)
        ))
        fwd_copies[-1].start()
    for t in range(1, n_cls):
        place_copies.append(push(
            places.at[pl.ds(half * cols, cols)], places_all.at[cls],
            place_send.at[t - 1], place_recv.at[t - 1], along(1, t),
        ))
        place_copies[-1].start()
    for copy in fwd_copies:
        copy.wait_recv()

    scores[...] = jnp.zeros_like(scores)

    def score_step(m, carry):
        at = pl.ds(pl.multiple_of(m * 512, 512), 512)
        scores[...] += lax.dot_general(
            rolled[:, at], refs_all[:, at], (((1,), (1,)), ((), ())),
            preferred_element_type=jnp.float32,
        )
        return carry

    lax.fori_loop(0, pix // 512, score_step, 0)

    lanes = 4 * class_count
    lane_block = lax.broadcasted_iota(jnp.int32, (part_count, lanes), 1) // class_count
    own_group = groups[...] == lane_block

    def spread(x):
        x = x + pltpu.roll(x, lanes // 2, 1)
        return x + pltpu.roll(x, lanes // 4, 1)

    packed = jnp.zeros((part_count, lanes), jnp.float32)
    for i in range(4):
        part = jnp.where(own_group, scores[i * part_count : (i + 1) * part_count, :], 0.0)
        packed = jnp.where(lane_block == i, spread(part), packed)
    last = spread(jnp.where(own_group, scores[4 * part_count :, :], 0.0))
    quarter = part_count // 4
    tail = jnp.zeros((quarter, lanes), jnp.float32)
    for b in range(4):
        tail = jnp.where(lane_block[:quarter] == b, last[b * quarter : (b + 1) * quarter], tail)
    score_box[vol, 0:part_count, :] = packed
    score_box[vol, part_count : part_count + quarter, :] = tail
    score_copies = []
    for t in range(1, n_vol):
        score_copies.append(push(
            score_box.at[vol], score_box.at[vol], score_send.at[t - 1], score_recv.at[t - 1], along(2, t)
        ))
        score_copies[-1].start()
    for copy in score_copies:
        copy.wait()
    summed = score_box[0]
    for v in range(1, n_vol):
        summed = summed + score_box[v]
    packed, tail = summed[:part_count], summed[part_count:]
    squares = []
    for i in range(4):
        part = spread(jnp.where(lane_block == i, packed, 0.0))
        squares.append(part * part)
    last = jnp.concatenate(
        [spread(jnp.where(lane_block[:quarter] == b, tail, 0.0)) for b in range(4)], axis=0
    )
    squares.append(last * last)
    total = squares[0]
    for i in range(1, SHIFTS):
        total = total + squares[i]
    mean_square = jnp.sum(total, axis=1, keepdims=True) * (1.0 / (4 * SHIFTS * class_count))
    for i in range(SHIFTS):
        weight = jnp.where(own_group, squares[i] / (mean_square + EPS_W), 0.0)
        flipped[:, i * part_count : (i + 1) * part_count] = weight.T.astype(jnp.bfloat16)

    tiles = pix // IMG // 4

    def sum_step(m, carry):
        block = lax.dot_general(
            flipped[...], rolled[:, pl.ds(pl.multiple_of(m * 4 * IMG, 4 * IMG), 4 * IMG)],
            (((1,), (0,)), ((), ())), preferred_element_type=jnp.float32,
        )
        for g in range(n_cls):
            tile = jnp.concatenate(
                [
                    block[g * class_count : (g + 1) * class_count, r * IMG : (r + 1) * IMG]
                    for r in range(4)
                ],
                axis=0,
            )
            at = pl.ds(pl.multiple_of((g * tiles + m) * IMG, IMG), IMG)
            by_col[:, at] = tile.T
        return carry

    lax.fori_loop(0, tiles, sum_step, 0, unroll=2)
    half_copy = push(
        by_col.at[pl.ds(other * cols, cols)], by_col_in, half_send.at[0], half_recv.at[0], along(0, 1)
    )
    half_copy.start()
    for copy in place_copies:
        copy.wait_recv()
    places32[cls] = places[pl.ds(pl.multiple_of(half * cols, cols), cols), :].astype(jnp.int32)
    for t in range(1, n_cls):
        source = lax.rem(cls - t + n_cls, n_cls)
        places32[source] = places_all[source].astype(jnp.int32)
    half_copy.wait()

    chunk = places.shape[1]
    low_ids = lax.broadcasted_iota(jnp.int32, (128, chunk), 0)
    high_ids = lax.broadcasted_iota(jnp.int32, (16, chunk), 0)

    def insert_eight(target, eight):
        base = pl.multiple_of(target * own_cols + eight * 8, 8)
        for j in range(8):
            total = jnp.zeros((64, 128), jnp.float32)
            for g in range(n_cls):
                span = slice(g * chunk, (g + 1) * chunk)
                place = places32[g, pl.ds(base, 8), :][j : j + 1]
                own = by_col[pl.ds(pl.multiple_of(half * cols + base, 8), 8), span][j : j + 1]
                got = by_col_in[pl.ds(base, 8), span][j : j + 1]
                hit = high_ids == (place >> 7)
                parts = []
                for value in (own, got):
                    coarse = value.astype(jnp.bfloat16).astype(jnp.float32)
                    fine = value - coarse
                    parts += [jnp.where(hit, coarse, 0.0), jnp.where(hit, fine, 0.0)]
                left = jnp.concatenate(parts, axis=0).astype(jnp.bfloat16)
                right = jnp.where(low_ids == (place & 127), 1.0, 0.0).astype(jnp.bfloat16)
                total += lax.dot_general(
                    left, right, (((1,), (1,)), ((), ())), preferred_element_type=jnp.float32
                )
            rows = pl.ds(pl.multiple_of(eight * 128 + j * 16, 16), 16)
            slab[target, 0, rows, :] = total[0:16] + total[16:32]
            slab[target, 1, rows, :] = total[32:48] + total[48:64]

    slab_copies = []
    for t in range(1, n_cls + 1):
        target = lax.rem(cls + t, n_cls)

        def eight_step(e, carry, target=target):
            insert_eight(target, e)
            return carry

        lax.fori_loop(0, own_cols // 8, eight_step, 0)
        if t < n_cls:
            slab_copies.append(push(
                slab.at[target], slab_in.at[t - 1], slab_send.at[t - 1], slab_recv.at[t - 1], along(1, t)
            ))
            slab_copies[-1].start()
    for copy in slab_copies:
        copy.wait()

    shell_ids = lax.broadcasted_iota(jnp.int32, (NSHELL, 128), 0)
    blank = jnp.zeros((1, 128), jnp.float32)

    def stat_step(m, carry):
        rows = pl.ds(pl.multiple_of(m * 8, 8), 8)
        maps = []
        for k in range(2):
            x = slab[cls, k, rows, :]
            for t in range(1, n_cls):
                x = x + slab_in[t - 1, k, rows, :]
            maps.append(x)
            slab[cls, k, rows, :] = x
        terms = []
        for x in (maps[0] * maps[0], maps[1] * maps[1], maps[0] * maps[1]):
            coarse = x.astype(jnp.bfloat16).astype(jnp.float32)
            terms += [coarse, x - coarse]
        shell = shells[rows, :]
        left = jnp.concatenate(
            [
                jnp.concatenate([x[j : j + 1] for x in terms] + [blank, blank], axis=0)
                for j in range(8)
            ],
            axis=1,
        ).astype(jnp.bfloat16)
        right = jnp.concatenate(
            [
                jnp.where(shell_ids == shell[j : j + 1], 1.0, 0.0).astype(jnp.bfloat16)
                for j in range(8)
            ],
            axis=1,
        )
        hot[m] = right
        return carry + lax.dot_general(
            left, right, (((1,), (1,)), ((), ())), preferred_element_type=jnp.float32
        )

    blocks = shells.shape[0] // 8
    sums = lax.fori_loop(0, blocks, stat_step, jnp.zeros((8, NSHELL), jnp.float32), unroll=4)
    mine_sq, other_sq, cross = sums[0:1] + sums[1:2], sums[2:3] + sums[3:4], sums[4:5] + sums[5:6]
    row_ids = lax.broadcasted_iota(jnp.int32, (8, NSHELL), 0)
    swap = jnp.full((1, NSHELL), half, jnp.int32) == 1
    first_sq = jnp.where(swap, other_sq, mine_sq)
    second_sq = jnp.where(swap, mine_sq, other_sq)
    stat = jnp.where(row_ids == 0, first_sq, jnp.where(row_ids == 1, second_sq, cross))
    at = 0
    for axis, box in enumerate((stat_half, stat_cls, stat_vol)):
        size = box.shape[0]
        box[mine[axis]] = stat
        copies = []
        for t in range(1, size):
            copies.append(push(
                box.at[mine[axis]], box.at[mine[axis]], stat_send.at[at], stat_recv.at[at], along(axis, t)
            ))
            copies[-1].start()
            at += 1
        for copy in copies:
            copy.wait()
        stat = box[0]
        for k in range(1, size):
            stat = stat + box[k]
    first_sq, second_sq, cross = stat[0:1], stat[1:2], stat[2:3]
    fsc = cross / (jnp.sqrt(first_sq) * jnp.sqrt(second_sq) + EPS_F)
    fsc_out[...] = fsc
    mean_sq = jnp.sum(first_sq + second_sq + 2.0 * cross, axis=1, keepdims=True) * (
        1.0 / (4.0 * n_vol * VOXS)
    )
    scale = 0.5 / jnp.sqrt(mean_sq + EPS_F)
    coarse = fsc.astype(jnp.bfloat16).astype(jnp.float32)
    pair = jnp.where(row_ids == 0, coarse, jnp.where(row_ids == 1, fsc - coarse, 0.0)).astype(jnp.bfloat16)

    def volume_step(m, carry):
        rows = pl.ds(pl.multiple_of(m * 8, 8), 8)
        picked = jnp.dot(pair, hot[m], preferred_element_type=jnp.float32)
        picked = picked[0:1] + picked[1:2]
        weight = jnp.concatenate([picked[:, j * 128 : (j + 1) * 128] for j in range(8)], axis=0)
        volume[rows, :] = weight * (slab[cls, 0, rows, :] + slab[cls, 1, rows, :]) * scale
        return carry

    lax.fori_loop(0, blocks, volume_step, 0, unroll=4)
    for copy in ref_copies + place_copies + fwd_copies:
        copy.wait_send()


def fused(images, groups, references, interp_index, shell_index):
    n_cls, n_vol = lax.axis_size("cls"), lax.axis_size("vol")
    part_count, pix = images.shape
    class_count = references.shape[0]
    rows = pix // IMG
    piece = shell_index.shape[1] // 128
    places = jnp.transpose(interp_index.astype(jnp.int16).reshape(class_count, rows, IMG), (2, 1, 0))
    places = places.reshape(IMG, rows * class_count)
    lanes = n_cls * class_count
    count = rows * class_count
    half_cols = IMG // 2
    dma = pltpu.SemaphoreType.DMA
    bf16, f32 = jnp.bfloat16, jnp.float32
    volume, fsc = pl.pallas_call(
        functools.partial(fused_body, n_cls, n_vol),
        out_shape=(
            jax.ShapeDtypeStruct((piece, 128), f32),
            jax.ShapeDtypeStruct((1, NSHELL), f32),
        ),
        in_specs=[pl.BlockSpec(memory_space=pltpu.VMEM)] * 5,
        out_specs=(pl.BlockSpec(memory_space=pltpu.VMEM),) * 2,
        scratch_shapes=[
            pltpu.VMEM((SHIFTS * part_count, pix), bf16),
            pltpu.VMEM((lanes, pix), bf16),
            pltpu.VMEM((n_cls, half_cols, count), jnp.int16),
            pltpu.VMEM((n_cls, half_cols, count), jnp.int32),
            pltpu.VMEM((SHIFTS * part_count, lanes), f32),
            pltpu.VMEM((n_vol, part_count + part_count // 4, lanes), f32),
            pltpu.VMEM((lanes, SHIFTS * part_count), bf16),
            pltpu.VMEM((IMG, n_cls * count), f32),
            pltpu.VMEM((half_cols, n_cls * count), f32),
            pltpu.VMEM((n_cls, 2, piece, 128), f32),
            pltpu.VMEM((n_cls - 1, 2, piece, 128), f32),
            pltpu.VMEM((piece // 8, NSHELL, 1024), bf16),
            pltpu.VMEM((2, 8, NSHELL), f32),
            pltpu.VMEM((n_cls, 8, NSHELL), f32),
            pltpu.VMEM((n_vol, 8, NSHELL), f32),
        ]
        + [dma((n_cls - 1,))] * 6
        + [dma((n_vol - 1,))] * 2
        + [dma((1,))] * 2
        + [dma((n_cls - 1,))] * 2
        + [dma((n_cls + n_vol - 1,))] * 2,
        compiler_params=pltpu.CompilerParams(
            collective_id=0, has_side_effects=True, vmem_limit_bytes=56 << 20
        ),
    )(images, references, places, groups, shell_index.reshape(piece, 128))
    return (volume.reshape(1, -1), fsc[0])


def shards(images, groups, references, interp_index, shell_index):
    n_cls = lax.axis_size("cls")
    n_vol = lax.axis_size("vol")
    n_half = lax.axis_size("half")
    part_count, pix_quarter = images.shape
    class_count = references.shape[0]
    if n_half == 2 and n_cls == 4 and class_count == 32:
        return fused(images, groups, references, interp_index, shell_index)
    capacity = max(2 * part_count // n_cls, 4)
    slot_count = n_cls * capacity
    owner_ids = groups[:, 0]
    same = owner_ids[:, None] == owner_ids[None, :]
    earlier = jnp.arange(part_count)[None, :] < jnp.arange(part_count)[:, None]
    order_in = jnp.sum((same & earlier).astype(jnp.int32), axis=1)
    slot_ids = owner_ids * capacity + order_in
    slot_hits = slot_ids[None, :] == jnp.arange(slot_count, dtype=jnp.int32)[:, None]
    source_ids = jnp.sum(
        jnp.where(slot_hits, jnp.arange(part_count, dtype=jnp.int32)[None, :], 0), axis=1
    )
    filled = jnp.any(slot_hits, axis=1)
    outgoing = jnp.where(
        filled[:, None], jnp.take(images, source_ids, axis=0), jnp.zeros((), jnp.bfloat16)
    )
    arrived = lax.all_to_all(
        outgoing.reshape(n_cls, capacity, pix_quarter),
        "cls",
        split_axis=0,
        concat_axis=0,
        tiled=True,
    )
    arrived = arrived.reshape(slot_count, pix_quarter)
    quarter_rows = pix_quarter // IMG
    shaped_refs = references.reshape(class_count, quarter_rows, IMG)
    rolled_refs = jnp.concatenate(
        [
            jnp.roll(shaped_refs, -(shift_id - SHIFTS // 2), axis=2).reshape(
                class_count, pix_quarter
            )
            for shift_id in range(SHIFTS)
        ],
        axis=0,
    )
    partial_scores = lax.dot_general(
        arrived, rolled_refs, (((1,), (1,)), ((), ())), preferred_element_type=jnp.float32
    )
    partial_scores = partial_scores.reshape(slot_count, SHIFTS, class_count)
    scores = lax.psum(partial_scores, "vol")
    squares = scores * scores
    mean_square = jnp.mean(squares, axis=(1, 2), keepdims=True)
    weights = (squares / (mean_square + EPS_W)).astype(jnp.bfloat16)
    weighted = lax.dot_general(
        weights.reshape(slot_count, SHIFTS * class_count),
        arrived,
        (((0,), (0,)), ((), ())),
        preferred_element_type=jnp.float32,
    )
    weighted = weighted.reshape(SHIFTS, class_count, quarter_rows, IMG)
    aligned = jnp.roll(weighted[0], -(SHIFTS // 2), axis=2)
    for shift_id in range(1, SHIFTS):
        aligned = aligned + jnp.roll(weighted[shift_id], shift_id - SHIFTS // 2, axis=2)
    by_column = jnp.transpose(interp_index.reshape(-1, IMG))
    slab_part = insert(by_column, jnp.transpose(aligned.reshape(-1, IMG)))
    piece_len = VOXS // (n_half * n_cls)
    slab_part = jnp.transpose(slab_part.reshape(n_half, n_cls, piece_len), (1, 0, 2)).reshape(-1)
    block_len = VOXS // n_cls
    slab_full = lax.psum(slab_part, "cls")
    own_block = lax.dynamic_slice_in_dim(slab_full, lax.axis_index("cls") * block_len, block_len)
    half_id = lax.axis_index("half")
    own_piece = lax.dynamic_slice_in_dim(own_block, half_id * piece_len, piece_len)
    other_piece = lax.dynamic_slice_in_dim(own_block, (1 - half_id) * piece_len, piece_len)
    mirror_piece = partner(other_piece, "half", 0)
    first = jnp.where(half_id == 0, own_piece, mirror_piece)
    second = jnp.where(half_id == 0, mirror_piece, own_piece)
    shell_hot = (shell_index[0][:, None] == jnp.arange(NSHELL, dtype=jnp.int32)[None, :]).astype(
        jnp.float32
    )
    stats = jnp.stack([first * first, second * second, first * second])
    shell_terms = jnp.dot(stats, shell_hot, precision=lax.Precision.HIGHEST)
    shell_sums = lax.psum(shell_terms, ("half", "cls", "vol"))
    shell_fsc = shell_sums[2] / (jnp.sqrt(shell_sums[0]) * jnp.sqrt(shell_sums[1]) + EPS_F)
    mean_sq = (jnp.sum(shell_sums[0]) + jnp.sum(shell_sums[1]) + 2.0 * jnp.sum(shell_sums[2])) / (
        4.0 * n_vol * VOXS
    )
    filter_vox = jnp.dot(shell_hot, shell_fsc, precision=lax.Precision.HIGHEST)
    volume = filter_vox * (0.5 * (first + second)) / jnp.sqrt(mean_sq + EPS_F)
    return (volume[None, :], shell_fsc)


def solution(mesh):
    placed = (
        P(("half", "cls"), "vol"),
        P(("half", "cls"), None),
        P("cls", "vol"),
        P("cls", "vol"),
        P("vol", ("half", "cls")),
    )
    return jax.shard_map(
        shards,
        mesh=mesh,
        in_specs=placed,
        out_specs=(P("vol", ("half", "cls")), P()),
        check_vma=False,
    )
```
